512 devices in a mesh: node: 16 (over z, core), rep: 32 (over x, y).
Axes of the slice: x: 4, y: 8, z: 8, core: 2. Of those that a mesh axis runs over, the one named last changes fastest.
Arguments:
- grads: bfloat16 [16, 32, 4096, 128], P('node', 'rep'), may hold values from -16 to 16, as said below
- feedback: bfloat16 [16, 32, 4096, 128], P('node', 'rep'), may hold values from -0.5 to 0.5, as said below
- master: float32 [4096, 128], P(('node', 'rep')), may hold values from -6 to 6
- moment: float32 [4096, 128], P(('node', 'rep')), may hold values from -0.75 to 0.75
- second: float32 [4096, 128], P(('node', 'rep')), may hold values from 0.0001 to 0.01
Outputs:
- fresh_feedback: bfloat16 [16, 32, 4096, 128], P('node', 'rep')
- mean_grad: float32 [4096, 128], P(('node', 'rep'))
- new_master: float32 [4096, 128], P(('node', 'rep'))
- new_moment: float32 [4096, 128], P(('node', 'rep'))
- new_second: float32 [4096, 128], P(('node', 'rep'))
- weights: bfloat16 [4096, 128], replicated
The draws below stay inside these ranges and needn't reach their ends.
Inputs may be any that keep to these rules, and one draw needn't show every extreme that they name: `grads`: every entry is a multiple of 1/16. `feedback`: every entry is a multiple of 1/128.
All inputs are finite; a program needn't handle non-finite values.
Results may differ from the reference program's by a relative error of at most 0.001.
Values may be sent and summed in bfloat16 or wider, within the bound.
A program may use at most 64 MiB of HBM per device.

```python
import math
import jax
import jax.numpy as jnp
import numpy as np
from jax import lax

BLOCK = 128
SHARD_ROWS = 8
NODE_DEVS = 16
REPLICAS = 32
ROWS = 4096


def summed_steps(key, shape, half):
    parts = jax.random.split(key, 4)
    total = jnp.zeros(shape, jnp.int32)
    for piece in parts:
        total = total + jax.random.randint(piece, shape, -half, half + 1)
    return total


def draw_grads(key, part):
    key = jax.random.fold_in(key, 11)
    first, other = jax.random.split(key)
    shape = (NODE_DEVS, REPLICAS, ROWS, BLOCK)
    steps_int = summed_steps(first, shape, 16)
    order = jax.random.permutation(other, REPLICAS)
    slot = jnp.arange(ROWS) // SHARD_ROWS % REPLICAS
    spike = slot[None, :] == order[:, None]
    factor = jnp.where(spike, 4.0, 1.0).astype(jnp.float32)
    return (steps_int.astype(jnp.float32) * factor[None, :, :, None] / 16.0).astype(jnp.bfloat16)


def draw_feedback(key, part):
    key = jax.random.fold_in(key, 23)
    shape = (NODE_DEVS, REPLICAS, ROWS, BLOCK)
    steps_int = summed_steps(key, shape, 16)
    return (steps_int.astype(jnp.float32) / 128.0).astype(jnp.bfloat16)


def shard_levels(rng, dims, cuts, smallest, high):
    level, own = 1.0, jax.random.fold_in(rng, 6)
    for dim, shards_of in cuts:
        heights = jnp.exp(jax.random.uniform(jax.random.fold_in(own, dim), (shards_of,), jnp.float32, smallest / len(cuts), high / len(cuts)))
        level = level * jnp.repeat(heights, dims[dim] // shards_of).reshape([-1 if axis == dim else 1 for axis in range(len(dims))])
    return level


def gaussian(key, dims, scale, limit, shards=(), held_as=jnp.bfloat16):
    factor_of = shard_levels(key, dims, shards, -0.22, 0.18) if shards else 1.0
    array = jax.random.normal(key, dims, jnp.float32) * scale * factor_of
    return jnp.minimum(jnp.maximum(array, -limit), limit).astype(held_as)


def setup_inputs(seed: int = 0) -> dict:
    arg_keys = jax.random.split(jax.random.key(seed), 6)
    return {
        "grads": draw_grads(jax.random.fold_in(arg_keys[5], 71), 0),
        "feedback": draw_feedback(jax.random.fold_in(arg_keys[5], 71), 0),
        "master": gaussian(arg_keys[2], (ROWS, BLOCK), 1.0, 6.0, ((0, 512),), jnp.float32),
        "moment": gaussian(arg_keys[3], (ROWS, BLOCK), 0.05, 0.75, ((0, 512),), jnp.float32),
        "second": jnp.clip(jnp.exp(math.log(0.01) - 4.6051702 * jax.random.uniform(arg_keys[4], (ROWS, BLOCK), jnp.float32) ** shard_levels(arg_keys[4], (ROWS, BLOCK), ((0, 512),), -0.2, 0.2)), 0.0001, 0.01),
    }


POWERS = np.power(2.0, np.arange(-24, 25))

def ceiling_scale(values):
    largest = lax.optimization_barrier(jnp.max(jnp.abs(values), axis=-1, keepdims=True))
    table = jnp.asarray(POWERS, dtype=jnp.float32)
    picked = jnp.where(table >= largest, table, table[-1])
    return lax.optimization_barrier(jnp.min(picked, axis=-1, keepdims=True)).astype(jnp.bfloat16)

def coded(values, levels, bound):
    scale_f = ceiling_scale(values).astype(jnp.float32)
    code = jnp.clip(jnp.floor(values / scale_f * levels + 0.5), -bound, bound).astype(jnp.bfloat16)
    return scale_f * code.astype(jnp.float32) / levels

def first_level(pair):
    local_grad, carried = pair
    summed = local_grad.astype(jnp.float32) + carried.astype(jnp.float32)
    decoded = coded(summed, 8.0, 7.0)
    return (lax.optimization_barrier(jnp.sum(decoded, axis=0)), (summed - decoded).astype(jnp.bfloat16))

def reference(grads, feedback, master, moment, second):
    partial_value, fresh = lax.map(first_level, (jnp.moveaxis(grads, 1, 0), jnp.moveaxis(feedback, 1, 0)))
    fresh_feedback = jnp.moveaxis(fresh, 0, 1)
    total = lax.optimization_barrier(jnp.sum(coded(partial_value, 8.0, 7.0), axis=0))
    mean_grad = total / (NODE_DEVS * REPLICAS)
    new_moment = 0.9 * moment + 0.1 * mean_grad
    new_second = 0.95 * second + 0.05 * mean_grad * mean_grad
    update = new_moment / 0.6513216 / (jnp.sqrt(new_second / 0.4012631) + 1e-08)
    new_master = master - 0.01 * (update + 0.1 * master)
    weights = coded(master, 128.0, 127.0).astype(jnp.bfloat16)
    return (fresh_feedback, mean_grad, new_master, new_moment, new_second, weights)
```

```python
import functools

import jax
import jax.numpy as jnp
from jax import lax
from jax.experimental import pallas as pl
from jax.experimental.pallas import tpu as pltpu
from jax.sharding import PartitionSpec as P

LANES = 128
MESH = pl.DeviceIdType.MESH
ONE_BIT = 1.5 * (1.0 - 2.0**-21)


def power_of(values):
    largest = jnp.max(jnp.abs(values), axis=-1, keepdims=True)
    raised = largest * ONE_BIT
    big = raised * float(2**23)
    return (raised + big) - big


def decoded_of(values, nudge):
    scale = power_of(values)
    magic = scale * float(1.5 * 2**20)
    bound = scale * 0.875
    rounded = ((values + nudge) + magic) - magic
    return jnp.minimum(jnp.maximum(rounded, -bound), bound)


def encode_master(values):
    largest = jnp.max(jnp.abs(values), axis=-1, keepdims=True)
    scale = jnp.full_like(largest, 2.0**24)
    inverse = jnp.full_like(largest, 2.0**-24)
    for k in range(23, -25, -1):
        fits = largest <= 2.0**k
        scale = jnp.where(fits, 2.0**k, scale)
        inverse = jnp.where(fits, 2.0**-k, inverse)
    code = jnp.floor(values * inverse * 128.0 + 0.5)
    code = jnp.minimum(jnp.maximum(code, -127.0), 127.0)
    return scale * code * (1.0 / 128.0)


def exchange(dims, g_hbm, f_hbm, master_ref, ff_ref, w_ref, total_ref,
             gbuf, fbuf, dbuf, sbuf, leaf, pay, out, ebuf, abuf,
             load_sem, sib_s, sib_r, leaf_s, leaf_r, pay_s, pay_r,
             az_s, az_r, ay_s, ay_r, ax_s, ax_r, ac_s, ac_r, two_s, two_r):
    Z, NX, NY, H = dims
    K = Z // 2
    R = NX * NY
    n = lax.axis_index("node")
    r = lax.axis_index("rep")
    z, c = n // 2, n % 2
    x, y = r // NY, r % NY
    oc = 1 - c

    def zoff(off):
        return lax.rem(z + off + Z, Z)

    def dev(off, core):
        return (zoff(off) * 2 + core, r)

    order = [K]
    for k in range(K - 1, 0, -1):
        order += [-k, k]
    order += [0]
    loads = {}
    for i, off in enumerate(order):
        d = zoff(off)
        loads[off] = [
            pltpu.make_async_copy(g_hbm.at[d], gbuf.at[d], load_sem.at[0, i]),
            pltpu.make_async_copy(f_hbm.at[d], fbuf.at[d], load_sem.at[1, i]),
        ]
        for cp in loads[off]:
            cp.start()

    barrier = pltpu.get_barrier_semaphore()
    for off in range(1, Z):
        pl.semaphore_signal(barrier, inc=1, device_id=dev(off, c), device_id_type=MESH)
    for off in (-1, 0, 1):
        pl.semaphore_signal(barrier, inc=1, device_id=dev(off, oc), device_id_type=MESH)

    def greet(i, carry):
        pl.semaphore_signal(barrier, inc=1, device_id=(n, lax.rem(r + i, R)), device_id_type=MESH)
        return carry

    lax.fori_loop(1, R, greet, 0)

    def encode(off):
        d = zoff(off)
        for cp in loads[off]:
            cp.wait()

        def body(i, carry):
            cc, h = i // 2, i % 2
            xv = gbuf[d, cc, h].astype(jnp.float32) + fbuf[d, cc, h].astype(jnp.float32)
            dec = decoded_of(xv, 2.0**-12)
            dbuf[d, cc, h] = dec.astype(jnp.bfloat16)
            ff_ref[d, cc, h] = (xv - dec).astype(jnp.bfloat16)
            return carry

        lax.fori_loop(0, 4, body, 0)

    waits = []

    def remote(src, dst, ssem, rsem, to):
        cp = pltpu.make_async_remote_copy(
            src_ref=src, dst_ref=dst, send_sem=ssem, recv_sem=rsem, device_id=to, device_id_type=MESH
        )
        cp.start()
        waits.append(cp)
        return cp

    w_ref[z, c, x, y] = encode_master(master_ref[...]).astype(jnp.bfloat16)
    encode(K)
    pl.semaphore_wait(barrier, (Z - 1) + 3 + (R - 1))

    def level(dr, h):
        return K if dr == h else K - 1

    def sgn(dr):
        return -1 if dr == 0 else 1

    def send_leaf(dr, h):
        d = zoff(sgn(dr) * level(dr, h))
        for cc in range(2):
            remote(dbuf.at[d, cc, h], leaf.at[dr, h, c], leaf_s.at[dr, h, cc], leaf_r.at[dr, h, c],
                   dev(sgn(dr), cc))

    sib = {}

    def send_sib(off, h=None):
        d = zoff(off)
        if h is None:
            src, dst = dbuf.at[d, oc], sbuf.at[d]
        else:
            src, dst = dbuf.at[d, oc, h], sbuf.at[d, h]
        sib[off] = remote(src, dst, sib_s.at[off + K], sib_r.at[off + K], dev(0, oc))

    sib_seen = set()

    def wait_sib(off):
        if off not in sib_seen:
            sib_seen.add(off)
            sib[off].wait_recv()

    def received(dr, h, k):
        if k + 1 == level(dr, h):
            for src in range(2):
                pltpu.make_async_copy(leaf.at[dr, h, src], leaf.at[dr, h, src], leaf_r.at[dr, h, src]).wait()
            return leaf[dr, h, 0].astype(jnp.float32) + leaf[dr, h, 1].astype(jnp.float32)
        pltpu.make_async_copy(pay.at[dr, h, k], pay.at[dr, h, k], pay_r.at[dr, h, k]).wait()
        return pay[dr, h, k]

    def send_pay(dr, h, k):
        off = sgn(dr) * k
        d = zoff(off)
        wait_sib(off)
        acc = dbuf[d, c, h].astype(jnp.float32) + sbuf[d, h].astype(jnp.float32)
        out[dr, h, k] = acc + received(dr, h, k)
        remote(out.at[dr, h, k], pay.at[dr, h, k - 1], pay_s.at[dr, h, k], pay_r.at[dr, h, k - 1],
               dev(sgn(dr), c))

    send_leaf(0, 0)
    send_leaf(1, 1)
    gz = [remote(w_ref.at[z, c, x, y], w_ref.at[z, c, x, y], az_s.at[off], az_r.at[off], dev(off, c))
          for off in range(1, Z)]
    encode(-(K - 1))
    send_leaf(0, 1)
    send_sib(-(K - 1), 0)
    encode(K - 1)
    send_leaf(1, 0)
    send_sib(K - 1, 1)
    for cp in gz:
        cp.wait_recv()
    gy = [remote(w_ref.at[:, c, x, y], w_ref.at[:, c, x, y], ay_s.at[off], ay_r.at[off],
                 (n, x * NY + lax.rem(y + off, NY))) for off in range(1, NY)]
    for k in range(K - 2, 0, -1):
        encode(-k)
        send_sib(-k)
        encode(k)
        send_sib(k)
    encode(0)
    send_sib(0)

    gx, gc = [], []
    for k in range(K - 1, 0, -1):
        for second in (True, False):
            for dr in range(2):
                h = dr if not second else 1 - dr
                if k < level(dr, h):
                    send_pay(dr, h, k)
        if k == K - 1:
            for cp in gy:
                cp.wait_recv()
            gx = [remote(w_ref.at[:, c, x], w_ref.at[:, c, x], ax_s.at[off], ax_r.at[off],
                         (n, lax.rem(x + off, NX) * NY + y)) for off in range(1, NX)]
            gc.append(remote(w_ref.at[:, c, x], w_ref.at[:, c, x], ac_s.at[0], ac_r.at[0], dev(0, oc)))

    G = R // 2
    wait_sib(0)
    for h in (1, 0):
        part = dbuf[z, c, h].astype(jnp.float32) + sbuf[z, h].astype(jnp.float32)
        part = part + received(0, h, 0) + received(1, h, 0)
        two = decoded_of(part, 2.0**-15)
        ebuf[h * G:(h + 1) * G] = two.reshape(G, 8, LANES).astype(jnp.bfloat16)

        def spread(i, carry):
            @pl.when(i != r)
            def _():
                pltpu.make_async_remote_copy(
                    src_ref=ebuf.at[i], dst_ref=abuf.at[r], send_sem=two_s, recv_sem=two_r,
                    device_id=(n, i), device_id_type=MESH).start()
            return carry

        lax.fori_loop(h * G, (h + 1) * G, spread, 0)

    for off, cp in enumerate(gx, 1):
        cp.wait_recv()
        xs = lax.rem(x - off + NX, NX)
        gc.append(remote(w_ref.at[:, c, xs], w_ref.at[:, c, xs], ac_s.at[off], ac_r.at[off], dev(0, oc)))

    abuf[r] = ebuf[r]
    rest = abuf.at[pl.ds(0, R - 1)]
    pltpu.make_async_copy(rest, rest, two_r).wait()
    total_ref[...] = jnp.sum(abuf[...].astype(jnp.float32), axis=0)
    for cp in gc:
        cp.wait_recv()
    for cp in waits:
        cp.wait_send()
    pltpu.make_async_copy(rest, rest, two_s).wait()


def finish(devices, total_ref, master_ref, moment_ref, second_ref, ff_in, w_in,
           ff_out, mean_ref, master_out, moment_out, second_out, w_out, sem):
    copies = [pltpu.make_async_copy(ff_in.at[i], ff_out.at[i], sem.at[0, i]) for i in range(ff_in.shape[0])]
    copies += [pltpu.make_async_copy(w_in.at[i], w_out.at[i], sem.at[1, i]) for i in range(w_in.shape[0])]
    for cp in copies:
        cp.start()
    mean = total_ref[...] * (1.0 / devices)
    moment = 0.9 * moment_ref[...] + 0.1 * mean
    second = 0.95 * second_ref[...] + 0.05 * mean * mean
    master = master_ref[...]
    update = moment / 0.6513216 / (jnp.sqrt(second / 0.4012631) + 1e-08)
    mean_ref[...] = mean
    moment_out[...] = moment
    second_out[...] = second
    master_out[...] = master - 0.01 * (update + 0.1 * master)
    for cp in copies:
        cp.wait()


def local(grads, feedback, master, moment, second):
    nodes, R = lax.axis_size("node"), lax.axis_size("rep")
    rows = grads.shape[2]
    Z = nodes // 2
    K = Z // 2
    NX = {32: 4, 4: 2}.get(R, 1)
    NY = R // NX
    H = rows // nodes // 2
    bf, f32 = jnp.bfloat16, jnp.float32
    blocks = (Z, 2, 2, H, LANES)
    wshape = (Z, 2, NX, NY, 8, LANES)
    any_, vmem = pl.BlockSpec(memory_space=pl.ANY), pl.BlockSpec(memory_space=pltpu.VMEM)
    dma = pltpu.SemaphoreType.DMA
    ff, weights, total = pl.pallas_call(
        functools.partial(exchange, (Z, NX, NY, H)),
        out_shape=(
            jax.ShapeDtypeStruct(blocks, bf),
            jax.ShapeDtypeStruct(wshape, bf),
            jax.ShapeDtypeStruct((8, LANES), f32),
        ),
        in_specs=[any_, any_, vmem],
        out_specs=(vmem, vmem, vmem),
        scratch_shapes=[
            pltpu.VMEM(blocks, bf),
            pltpu.VMEM(blocks, bf),
            pltpu.VMEM(blocks, bf),
            pltpu.VMEM((Z, 2, H, LANES), bf),
            pltpu.VMEM((2, 2, 2, H, LANES), bf),
            pltpu.VMEM((2, 2, K, H, LANES), f32),
            pltpu.VMEM((2, 2, K, H, LANES), f32),
            pltpu.VMEM((R, 8, LANES), bf),
            pltpu.VMEM((R, 8, LANES), bf),
            dma((2, Z)),
            dma((Z + 1,)), dma((Z + 1,)),
            dma((2, 2, 2)), dma((2, 2, 2)),
            dma((2, 2, K)), dma((2, 2, K)),
            dma((Z,)), dma((Z,)),
            dma((NY,)), dma((NY,)),
            dma((NX,)), dma((NX,)),
            dma((NX,)), dma((NX,)),
            dma, dma,
        ],
        compiler_params=pltpu.CompilerParams(
            collective_id=0, has_side_effects=True, vmem_limit_bytes=32 * 2**20
        ),
        cost_estimate=pl.CostEstimate(flops=20 * rows * LANES, bytes_accessed=10 * rows * LANES, transcendentals=0),
        name="exchange",
    )(grads.reshape(blocks), feedback.reshape(blocks), master)
    small = jax.ShapeDtypeStruct((8, LANES), f32)
    ff, mean, new_master, new_moment, new_second, weights = pl.pallas_call(
        functools.partial(finish, nodes * R),
        out_shape=(jax.ShapeDtypeStruct(blocks, bf), small, small, small, small, jax.ShapeDtypeStruct(wshape, bf)),
        in_specs=[vmem] * 4 + [any_] * 2,
        out_specs=(any_, vmem, vmem, vmem, vmem, any_),
        scratch_shapes=[dma((2, Z))],
        cost_estimate=pl.CostEstimate(flops=20 * 8 * LANES, bytes_accessed=8 * rows * LANES, transcendentals=0),
        name="finish",
    )(total, master, moment, second, ff, weights)
    return (ff.reshape(grads.shape), mean, new_master, new_moment, new_second, weights.reshape(rows, LANES))


def solution(mesh):
    each, shard = P("node", "rep", None, None), P(("node", "rep"), None)
    return jax.shard_map(
        local,
        mesh=mesh,
        in_specs=(each, each, shard, shard, shard),
        out_specs=(each, shard, shard, shard, shard, P()),
        check_vma=False,
    )
```

```python
import functools

import jax
import jax.numpy as jnp
from jax import lax
from jax.experimental import pallas as pl
from jax.experimental.pallas import tpu as pltpu
from jax.sharding import PartitionSpec as P

LANES = 128
MESH = pl.DeviceIdType.MESH
ONE_BIT = 1.5 * (1.0 - 2.0**-21)


def power_of(values):
    largest = jnp.max(jnp.abs(values), axis=-1, keepdims=True)
    raised = largest * ONE_BIT
    big = raised * float(2**23)
    return (raised + big) - big


def decoded_of(values, nudge):
    scale = power_of(values)
    magic = scale * float(1.5 * 2**20)
    bound = scale * 0.875
    rounded = ((values + nudge) + magic) - magic
    return jnp.minimum(jnp.maximum(rounded, -bound), bound)


def encode_master(values):
    largest = jnp.max(jnp.abs(values), axis=-1, keepdims=True)
    scale = jnp.full_like(largest, 2.0**24)
    inverse = jnp.full_like(largest, 2.0**-24)
    for k in range(23, -25, -1):
        fits = largest <= 2.0**k
        scale = jnp.where(fits, 2.0**k, scale)
        inverse = jnp.where(fits, 2.0**-k, inverse)
    code = jnp.floor(values * inverse * 128.0 + 0.5)
    code = jnp.minimum(jnp.maximum(code, -127.0), 127.0)
    return scale * code * (1.0 / 128.0)


def exchange(dims, g_hbm, f_hbm, master_hbm, moment_hbm, second_hbm, ff_ref, w_ref, small_ref,
             gbuf, fbuf, dbuf, sbuf, leaf, pay, out, ebuf, abuf, state,
             state_sem, load_sem, sib_s, sib_r, leaf_s, leaf_r, pay_s, pay_r,
             az_s, az_r, ay_s, ay_r, ax_s, ax_r, ac_s, ac_r, two_s, two_r):
    Z, NX, NY, H = dims
    K = Z // 2
    R = NX * NY
    n = lax.axis_index("node")
    r = lax.axis_index("rep")
    z, c = n // 2, n % 2
    x, y = r // NY, r % NY
    oc = 1 - c

    def zoff(off):
        return lax.rem(z + off + Z, Z)

    def dev(off, core):
        return (zoff(off) * 2 + core, r)

    states = [pltpu.make_async_copy(ref, state.at[i], state_sem.at[i])
              for i, ref in enumerate((master_hbm, moment_hbm, second_hbm))]
    for cp in states:
        cp.start()
    order = [K]
    for k in range(K - 1, 0, -1):
        order += [-k, k]
    order += [0]
    loads = {}
    for i, off in enumerate(order):
        d = zoff(off)
        loads[off] = [
            pltpu.make_async_copy(g_hbm.at[d], gbuf.at[d], load_sem.at[0, i]),
            pltpu.make_async_copy(f_hbm.at[d], fbuf.at[d], load_sem.at[1, i]),
        ]
        for cp in loads[off]:
            cp.start()

    barrier = pltpu.get_barrier_semaphore()
    for off in range(1, Z):
        pl.semaphore_signal(barrier, inc=1, device_id=dev(off, c), device_id_type=MESH)
    for off in (-1, 0, 1):
        pl.semaphore_signal(barrier, inc=1, device_id=dev(off, oc), device_id_type=MESH)

    def greet(i, carry):
        pl.semaphore_signal(barrier, inc=1, device_id=(n, lax.rem(r + i, R)), device_id_type=MESH)
        return carry

    lax.fori_loop(1, R, greet, 0)

    def encode(off):
        d = zoff(off)
        for cp in loads[off]:
            cp.wait()

        def body(i, carry):
            cc, h = i // 2, i % 2
            xv = gbuf[d, cc, h].astype(jnp.float32) + fbuf[d, cc, h].astype(jnp.float32)
            dec = decoded_of(xv, 2.0**-12)
            dbuf[d, cc, h] = dec.astype(jnp.bfloat16)
            ff_ref[d, cc, h] = (xv - dec).astype(jnp.bfloat16)
            return carry

        lax.fori_loop(0, 4, body, 0)

    waits = []

    def remote(src, dst, ssem, rsem, to):
        cp = pltpu.make_async_remote_copy(
            src_ref=src, dst_ref=dst, send_sem=ssem, recv_sem=rsem, device_id=to, device_id_type=MESH
        )
        cp.start()
        waits.append(cp)
        return cp

    for cp in states:
        cp.wait()
    w_ref[z, c, x, y] = encode_master(state[0]).astype(jnp.bfloat16)
    encode(K)
    pl.semaphore_wait(barrier, (Z - 1) + 3 + (R - 1))

    def level(dr, h):
        return K if dr == h else K - 1

    def sgn(dr):
        return -1 if dr == 0 else 1

    def send_leaf(dr, h):
        d = zoff(sgn(dr) * level(dr, h))
        for cc in range(2):
            remote(dbuf.at[d, cc, h], leaf.at[dr, h, c], leaf_s.at[dr, h, cc], leaf_r.at[dr, h, c],
                   dev(sgn(dr), cc))

    sib = {}

    def send_sib(off, h=None):
        d = zoff(off)
        if h is None:
            src, dst = dbuf.at[d, oc], sbuf.at[d]
        else:
            src, dst = dbuf.at[d, oc, h], sbuf.at[d, h]
        sib[off] = remote(src, dst, sib_s.at[off + K], sib_r.at[off + K], dev(0, oc))

    sib_seen = set()

    def wait_sib(off):
        if off not in sib_seen:
            sib_seen.add(off)
            sib[off].wait_recv()

    def received(dr, h, k):
        if k + 1 == level(dr, h):
            for src in range(2):
                pltpu.make_async_copy(leaf.at[dr, h, src], leaf.at[dr, h, src], leaf_r.at[dr, h, src]).wait()
            return leaf[dr, h, 0].astype(jnp.float32) + leaf[dr, h, 1].astype(jnp.float32)
        pltpu.make_async_copy(pay.at[dr, h, k], pay.at[dr, h, k], pay_r.at[dr, h, k]).wait()
        return pay[dr, h, k]

    def send_pay(dr, h, k):
        off = sgn(dr) * k
        d = zoff(off)
        wait_sib(off)
        acc = dbuf[d, c, h].astype(jnp.float32) + sbuf[d, h].astype(jnp.float32)
        out[dr, h, k] = acc + received(dr, h, k)
        remote(out.at[dr, h, k], pay.at[dr, h, k - 1], pay_s.at[dr, h, k], pay_r.at[dr, h, k - 1],
               dev(sgn(dr), c))

    send_leaf(0, 0)
    send_leaf(1, 1)
    gz = [remote(w_ref.at[z, c, x, y], w_ref.at[z, c, x, y], az_s.at[off], az_r.at[off], dev(off, c))
          for off in range(1, Z)]
    encode(-(K - 1))
    send_leaf(0, 1)
    send_sib(-(K - 1), 0)
    encode(K - 1)
    send_leaf(1, 0)
    send_sib(K - 1, 1)
    for cp in gz:
        cp.wait_recv()
    gy = [remote(w_ref.at[:, c, x, y], w_ref.at[:, c, x, y], ay_s.at[off], ay_r.at[off],
                 (n, x * NY + lax.rem(y + off, NY))) for off in range(1, NY)]
    for k in range(K - 2, 0, -1):
        encode(-k)
        send_sib(-k)
        encode(k)
        send_sib(k)
    encode(0)
    send_sib(0)

    gx, gc = [], []
    for k in range(K - 1, 0, -1):
        for second in (True, False):
            for dr in range(2):
                h = dr if not second else 1 - dr
                if k < level(dr, h):
                    send_pay(dr, h, k)
        if k == K - 1:
            for cp in gy:
                cp.wait_recv()
            gx = [remote(w_ref.at[:, c, x], w_ref.at[:, c, x], ax_s.at[off], ax_r.at[off],
                         (n, lax.rem(x + off, NX) * NY + y)) for off in range(1, NX)]
            gc.append(remote(w_ref.at[:, c, x], w_ref.at[:, c, x], ac_s.at[0], ac_r.at[0], dev(0, oc)))

    G = R // 2
    wait_sib(0)
    for h in (1, 0):
        part = dbuf[z, c, h].astype(jnp.float32) + sbuf[z, h].astype(jnp.float32)
        part = part + received(0, h, 0) + received(1, h, 0)
        two = decoded_of(part, 2.0**-15)
        ebuf[h * G:(h + 1) * G] = two.reshape(G, 8, LANES).astype(jnp.bfloat16)

        def spread(i, carry):
            @pl.when(i != r)
            def _():
                pltpu.make_async_remote_copy(
                    src_ref=ebuf.at[i], dst_ref=abuf.at[r], send_sem=two_s, recv_sem=two_r,
                    device_id=(n, i), device_id_type=MESH).start()
            return carry

        lax.fori_loop(h * G, (h + 1) * G, spread, 0)

    for off, cp in enumerate(gx, 1):
        cp.wait_recv()
        xs = lax.rem(x - off + NX, NX)
        gc.append(remote(w_ref.at[:, c, xs], w_ref.at[:, c, xs], ac_s.at[off], ac_r.at[off], dev(0, oc)))

    abuf[r] = ebuf[r]
    rest = abuf.at[pl.ds(0, R - 1)]
    pltpu.make_async_copy(rest, rest, two_r).wait()
    mean = jnp.sum(abuf[...].astype(jnp.float32), axis=0) * (1.0 / (2 * Z * R))
    master = state[0]
    moment = 0.9 * state[1] + 0.1 * mean
    second = 0.95 * state[2] + 0.05 * mean * mean
    update = moment / 0.6513216 / (jnp.sqrt(second / 0.4012631) + 1e-08)
    small_ref[0] = mean
    small_ref[1] = master - 0.01 * (update + 0.1 * master)
    small_ref[2] = moment
    small_ref[3] = second
    for cp in gc:
        cp.wait_recv()
    for cp in waits:
        cp.wait_send()
    pltpu.make_async_copy(rest, rest, two_s).wait()


def finish(small_ref, ff_in, w_in, ff_out, mean_out, master_out, moment_out, second_out, w_out, sem):
    copies = [pltpu.make_async_copy(ff_in, ff_out, sem.at[4]), pltpu.make_async_copy(w_in, w_out, sem.at[5])]
    copies += [pltpu.make_async_copy(small_ref.at[i], out, sem.at[i])
               for i, out in enumerate((mean_out, master_out, moment_out, second_out))]
    for cp in copies:
        cp.start()
    for cp in copies:
        cp.wait()


def local(grads, feedback, master, moment, second):
    nodes, R = lax.axis_size("node"), lax.axis_size("rep")
    rows = grads.shape[2]
    Z = nodes // 2
    K = Z // 2
    NX = {32: 4, 4: 2}.get(R, 1)
    NY = R // NX
    H = rows // nodes // 2
    bf, f32 = jnp.bfloat16, jnp.float32
    blocks = (Z, 2, 2, H, LANES)
    wshape = (Z, 2, NX, NY, 8, LANES)
    hbm, vmem = pl.BlockSpec(memory_space=pltpu.HBM), pl.BlockSpec(memory_space=pltpu.VMEM)
    dma = pltpu.SemaphoreType.DMA
    ff, weights, small = pl.pallas_call(
        functools.partial(exchange, (Z, NX, NY, H)),
        out_shape=(
            jax.ShapeDtypeStruct(blocks, bf),
            jax.ShapeDtypeStruct(wshape, bf),
            jax.ShapeDtypeStruct((4, 8, LANES), f32),
        ),
        in_specs=[hbm] * 5,
        out_specs=(vmem, vmem, vmem),
        scratch_shapes=[
            pltpu.VMEM(blocks, bf),
            pltpu.VMEM(blocks, bf),
            pltpu.VMEM(blocks, bf),
            pltpu.VMEM((Z, 2, H, LANES), bf),
            pltpu.VMEM((2, 2, 2, H, LANES), bf),
            pltpu.VMEM((2, 2, K, H, LANES), f32),
            pltpu.VMEM((2, 2, K, H, LANES), f32),
            pltpu.VMEM((R, 8, LANES), bf),
            pltpu.VMEM((R, 8, LANES), bf),
            pltpu.VMEM((3, 8, LANES), f32),
            dma((3,)),
            dma((2, Z)),
            dma((Z + 1,)), dma((Z + 1,)),
            dma((2, 2, 2)), dma((2, 2, 2)),
            dma((2, 2, K)), dma((2, 2, K)),
            dma((Z,)), dma((Z,)),
            dma((NY,)), dma((NY,)),
            dma((NX,)), dma((NX,)),
            dma((NX,)), dma((NX,)),
            dma, dma,
        ],
        compiler_params=pltpu.CompilerParams(
            collective_id=0, has_side_effects=True, vmem_limit_bytes=32 * 2**20
        ),
        cost_estimate=pl.CostEstimate(flops=20 * rows * LANES, bytes_accessed=10 * rows * LANES, transcendentals=0),
        name="exchange",
    )(grads.reshape(blocks), feedback.reshape(blocks), master, moment, second)
    shard = jax.ShapeDtypeStruct((8, LANES), f32)
    ff, mean, new_master, new_moment, new_second, weights = pl.pallas_call(
        finish,
        out_shape=(jax.ShapeDtypeStruct(blocks, bf), shard, shard, shard, shard, jax.ShapeDtypeStruct(wshape, bf)),
        in_specs=[vmem] * 3,
        out_specs=(hbm,) * 6,
        scratch_shapes=[dma((6,))],
        compiler_params=pltpu.CompilerParams(vmem_limit_bytes=8 * 2**20),
        cost_estimate=pl.CostEstimate(flops=0, bytes_accessed=8 * rows * LANES, transcendentals=0),
        name="finish",
    )(small, ff, weights)
    return (ff.reshape(grads.shape), mean, new_master, new_moment, new_second, weights.reshape(rows, LANES))


def solution(mesh):
    each, shard = P("node", "rep", None, None), P(("node", "rep"), None)
    return jax.shard_map(
        local,
        mesh=mesh,
        in_specs=(each, each, shard, shard, shard),
        out_specs=(each, shard, shard, shard, shard, P()),
        check_vma=False,
    )
```

```python
import functools

import jax
import jax.numpy as jnp
from jax import lax
from jax.experimental import pallas as pl
from jax.experimental.pallas import tpu as pltpu
from jax.sharding import PartitionSpec as P

LANES = 128
MESH = pl.DeviceIdType.MESH
ONE_BIT = 1.5 * (1.0 - 2.0**-21)


def power_of(values):
    largest = jnp.max(jnp.abs(values), axis=-1, keepdims=True)
    raised = largest * ONE_BIT
    big = raised * float(2**23)
    return (raised + big) - big


def decoded_of(values, nudge):
    scale = power_of(values)
    magic = scale * float(1.5 * 2**20)
    bound = scale * 0.875
    rounded = ((values + nudge) + magic) - magic
    return jnp.minimum(jnp.maximum(rounded, -bound), bound)


def encode_master(values):
    largest = jnp.max(jnp.abs(values), axis=-1, keepdims=True)
    scale = jnp.full_like(largest, 2.0**24)
    inverse = jnp.full_like(largest, 2.0**-24)
    for k in range(23, -25, -1):
        fits = largest <= 2.0**k
        scale = jnp.where(fits, 2.0**k, scale)
        inverse = jnp.where(fits, 2.0**-k, inverse)
    code = jnp.floor(values * inverse * 128.0 + 0.5)
    code = jnp.minimum(jnp.maximum(code, -127.0), 127.0)
    return scale * code * (1.0 / 128.0)


def exchange(dims, g_hbm, f_hbm, master_hbm, ff_ref, w_ref, total_ref,
             gbuf, fbuf, dbuf, sbuf, leaf, pay, out, ebuf, abuf, state,
             state_sem, load_sem, sib_s, sib_r, leaf_s, leaf_r, pay_s, pay_r,
             az_s, az_r, ay_s, ay_r, ax_s, ax_r, ac_s, ac_r, two_s, two_r):
    Z, NX, NY, H = dims
    K = Z // 2
    R = NX * NY
    n = lax.axis_index("node")
    r = lax.axis_index("rep")
    z, c = n // 2, n % 2
    x, y = r // NY, r % NY
    oc = 1 - c

    def zoff(off):
        return lax.rem(z + off + Z, Z)

    def dev(off, core):
        return (zoff(off) * 2 + core, r)

    master_copy = pltpu.make_async_copy(master_hbm, state, state_sem)
    master_copy.start()
    order = [K]
    for k in range(K - 1, 0, -1):
        order += [-k, k]
    order += [0]
    loads = {}

    def load(offs):
        for off in offs:
            d, i = zoff(off), off + K
            loads[off] = [
                pltpu.make_async_copy(g_hbm.at[d], gbuf.at[d], load_sem.at[0, i]),
                pltpu.make_async_copy(f_hbm.at[d], fbuf.at[d], load_sem.at[1, i]),
            ]
            for cp in loads[off]:
                cp.start()

    barrier = pltpu.get_barrier_semaphore()
    load(order[:1])
    for off in range(1, Z):
        pl.semaphore_signal(barrier, inc=1, device_id=dev(off, c), device_id_type=MESH)
    for off in (-1, 0, 1):
        pl.semaphore_signal(barrier, inc=1, device_id=dev(off, oc), device_id_type=MESH)
    load(order[1:3])

    def greet(i, carry):
        pl.semaphore_signal(barrier, inc=1, device_id=(n, lax.rem(r + i, R)), device_id_type=MESH)
        return carry

    lax.fori_loop(1, R, greet, 0)
    load(order[3:])

    def encode(off):
        d = zoff(off)
        for cp in loads[off]:
            cp.wait()

        xv = gbuf[d].astype(jnp.float32) + fbuf[d].astype(jnp.float32)
        dec = decoded_of(xv, 2.0**-12)
        dbuf[d] = dec.astype(jnp.bfloat16)
        ff_ref[d] = (xv - dec).astype(jnp.bfloat16)

    waits = []

    def remote(src, dst, ssem, rsem, to):
        cp = pltpu.make_async_remote_copy(
            src_ref=src, dst_ref=dst, send_sem=ssem, recv_sem=rsem, device_id=to, device_id_type=MESH
        )
        cp.start()
        waits.append(cp)
        return cp

    def level(dr, h):
        return K if dr == h else K - 1

    def sgn(dr):
        return -1 if dr == 0 else 1

    flying = {0: [], 1: []}

    def pace(dr):
        flying[dr] = []

    def send_leaf(dr, h):
        d = zoff(sgn(dr) * level(dr, h))
        pace(dr)
        for cc in range(2):
            flying[dr].append(remote(dbuf.at[d, cc, h], leaf.at[dr, h, c], leaf_s.at[dr, h, cc], leaf_r.at[dr, h, c],
                                     dev(sgn(dr), cc)))

    sib = {}

    def send_sib(off, h=None):
        d = zoff(off)
        if h is None:
            src, dst = dbuf.at[d, oc], sbuf.at[d]
        else:
            src, dst = dbuf.at[d, oc, h], sbuf.at[d, h]
        sib[off] = remote(src, dst, sib_s.at[off + K], sib_r.at[off + K], dev(0, oc))

    sib_seen = set()

    def wait_sib(off):
        if off not in sib_seen:
            sib_seen.add(off)
            sib[off].wait_recv()

    def received(dr, h, k):
        if k + 1 == level(dr, h):
            for src in range(2):
                pltpu.make_async_copy(leaf.at[dr, h, src], leaf.at[dr, h, src], leaf_r.at[dr, h, src]).wait()
            return leaf[dr, h, 0].astype(jnp.float32) + leaf[dr, h, 1].astype(jnp.float32)
        pltpu.make_async_copy(pay.at[dr, h, k], pay.at[dr, h, k], pay_r.at[dr, h, k]).wait()
        return pay[dr, h, k]

    def send_pay(dr, h, k):
        off = sgn(dr) * k
        d = zoff(off)
        wait_sib(off)
        acc = dbuf[d, c, h].astype(jnp.float32) + sbuf[d, h].astype(jnp.float32)
        out[dr, h, k] = acc + received(dr, h, k)
        pace(dr)
        flying[dr].append(remote(out.at[dr, h, k], pay.at[dr, h, k - 1], pay_s.at[dr, h, k],
                                 pay_r.at[dr, h, k - 1], dev(sgn(dr), c)))

    master_copy.wait()
    w_ref[z, c, x, y] = encode_master(state[...]).astype(jnp.bfloat16)
    encode(K)
    pl.semaphore_wait(barrier, (Z - 1) + 3 + (R - 1))
    gz = [remote(w_ref.at[z, c, x, y], w_ref.at[z, c, x, y], az_s.at[off], az_r.at[off], dev(off, c))
          for off in range(1, Z)]
    send_leaf(0, 0)
    send_leaf(1, 1)
    encode(-(K - 1))
    send_sib(-(K - 1), 0)
    encode(K - 1)
    send_sib(K - 1, 1)
    for k in range(K - 2, 0, -1):
        encode(-k)
        send_sib(-k)
        encode(k)
        send_sib(k)
    encode(0)
    send_sib(0)
    send_leaf(0, 1)
    send_leaf(1, 0)
    for cp in gz:
        cp.wait_recv()
    gy = [remote(w_ref.at[:, c, x, y], w_ref.at[:, c, x, y], ay_s.at[off], ay_r.at[off],
                 (n, x * NY + lax.rem(y + off, NY))) for off in range(1, NY)]

    def weights_x(stage):
        def to(off):
            return (n, lax.rem(x + off + NX, NX) * NY + y)

        def piece(off, part):
            return w_ref.at[part, c, lax.rem(x + off + NX, NX)]

        full = pl.ds(0, Z)
        if stage == 0:
            for cp in gy:
                cp.wait_recv()
            for i, off in enumerate((1, -1) if NX > 2 else (1,) if NX > 1 else ()):
                gx.append(remote(piece(0, full), piece(0, full), ax_s.at[i], ax_r.at[i], to(off)))
            to_sibling(piece(0, full), 0)
        if stage == 1:
            for i, off in enumerate((1, -1) if NX > 2 else (1,) if NX > 1 else ()):
                gx[i].wait_recv()
                if NX > 2:
                    half = piece(-off, pl.ds(i * Z // 2, Z // 2))
                    gx.append(remote(half, half, ax_s.at[2 + i], ax_r.at[2 + i], to(off)))
                to_sibling(piece(-off, full), 1 + i)
        if stage == 2 and NX > 2:
            for cp in gx[2:]:
                cp.wait_recv()
            to_sibling(piece(2, full), 3)

    def to_sibling(ref, i):
        gc.append(remote(ref, ref, ac_s.at[i], ac_r.at[i], dev(0, oc)))

    gx, gc = [], []
    for k in range(K - 1, 0, -1):
        for second in (True, False):
            for dr in range(2):
                h = dr if not second else 1 - dr
                if k < level(dr, h):
                    send_pay(dr, h, k)
            if k == 1 and second:
                weights_x(0)

    G = R // 2
    wait_sib(0)
    for h in (1, 0):
        part = dbuf[z, c, h].astype(jnp.float32) + sbuf[z, h].astype(jnp.float32)
        part = part + received(0, h, 0) + received(1, h, 0)
        two = decoded_of(part, 2.0**-15)
        ebuf[h * G:(h + 1) * G] = two.reshape(G, 8, LANES).astype(jnp.bfloat16)

        for j in range(NY):
            dy = NY // 2 + (1 - 2 * (j % 2)) * ((j + 1) // 2)
            for i in range(NX // 2):
                to = (h * NX // 2 + i) * NY + lax.rem(y + dy, NY)

                def send():
                    pltpu.make_async_remote_copy(
                        src_ref=ebuf.at[to], dst_ref=abuf.at[r], send_sem=two_s, recv_sem=two_r,
                        device_id=(n, to), device_id_type=MESH).start()

                if dy == 0:
                    pl.when(to != r)(send)
                else:
                    send()

    weights_x(1)
    abuf[r] = ebuf[r]
    rest = abuf.at[pl.ds(0, R - 1)]
    pltpu.make_async_copy(rest, rest, two_r).wait()
    total_ref[...] = jnp.sum(abuf[...].astype(jnp.float32), axis=0)
    weights_x(2)
    for cp in gc:
        cp.wait_recv()
    for cp in waits:
        cp.wait_send()
    pltpu.make_async_copy(rest, rest, two_s).wait()


def finish(devices, total_ref, master_ref, moment_ref, second_ref, ff_in, w_in,
           ff_out, mean_out, master_out, moment_out, second_out, w_out, small, sem):
    copies = [pltpu.make_async_copy(ff_in, ff_out, sem.at[4]), pltpu.make_async_copy(w_in, w_out, sem.at[5])]
    for cp in copies:
        cp.start()
    mean = total_ref[...] * (1.0 / devices)
    master = master_ref[...]
    moment = 0.9 * moment_ref[...] + 0.1 * mean
    second = 0.95 * second_ref[...] + 0.05 * mean * mean
    update = moment / 0.6513216 / (jnp.sqrt(second / 0.4012631) + 1e-08)
    small[0] = mean
    small[1] = master - 0.01 * (update + 0.1 * master)
    small[2] = moment
    small[3] = second
    for i, out in enumerate((mean_out, master_out, moment_out, second_out)):
        copies.append(pltpu.make_async_copy(small.at[i], out, sem.at[i]))
        copies[-1].start()
    for cp in copies:
        cp.wait()


def local(grads, feedback, master, moment, second):
    nodes, R = lax.axis_size("node"), lax.axis_size("rep")
    rows = grads.shape[2]
    Z = nodes // 2
    K = Z // 2
    NX = {32: 4, 4: 2}.get(R, 1)
    NY = R // NX
    H = rows // nodes // 2
    bf, f32 = jnp.bfloat16, jnp.float32
    blocks = (Z, 2, 2, H, LANES)
    wshape = (Z, 2, NX, NY, 8, LANES)
    hbm, vmem = pl.BlockSpec(memory_space=pltpu.HBM), pl.BlockSpec(memory_space=pltpu.VMEM)
    dma = pltpu.SemaphoreType.DMA
    ff, weights, total = pl.pallas_call(
        functools.partial(exchange, (Z, NX, NY, H)),
        out_shape=(
            jax.ShapeDtypeStruct(blocks, bf),
            jax.ShapeDtypeStruct(wshape, bf),
            jax.ShapeDtypeStruct((8, LANES), f32),
        ),
        in_specs=[hbm] * 3,
        out_specs=(vmem, vmem, vmem),
        scratch_shapes=[
            pltpu.VMEM(blocks, bf),
            pltpu.VMEM(blocks, bf),
            pltpu.VMEM(blocks, bf),
            pltpu.VMEM((Z, 2, H, LANES), bf),
            pltpu.VMEM((2, 2, 2, H, LANES), bf),
            pltpu.VMEM((2, 2, K, H, LANES), f32),
            pltpu.VMEM((2, 2, K, H, LANES), f32),
            pltpu.VMEM((R, 8, LANES), bf),
            pltpu.VMEM((R, 8, LANES), bf),
            pltpu.VMEM((8, LANES), f32),
            dma,
            dma((2, Z + 1)),
            dma((Z + 1,)), dma((Z + 1,)),
            dma((2, 2, 2)), dma((2, 2, 2)),
            dma((2, 2, K)), dma((2, 2, K)),
            dma((Z,)), dma((Z,)),
            dma((NY,)), dma((NY,)),
            dma((4,)), dma((4,)),
            dma((4,)), dma((4,)),
            dma, dma,
        ],
        compiler_params=pltpu.CompilerParams(
            collective_id=0, has_side_effects=True, vmem_limit_bytes=51 * 2**20 + 2**19
        ),
        cost_estimate=pl.CostEstimate(flops=20 * rows * LANES, bytes_accessed=10 * rows * LANES, transcendentals=0),
        name="exchange",
    )(grads.reshape(blocks), feedback.reshape(blocks), master)
    shard = jax.ShapeDtypeStruct((8, LANES), f32)
    ff, mean, new_master, new_moment, new_second, weights = pl.pallas_call(
        functools.partial(finish, nodes * R),
        out_shape=(jax.ShapeDtypeStruct(blocks, bf), shard, shard, shard, shard, jax.ShapeDtypeStruct(wshape, bf)),
        in_specs=[vmem] * 6,
        out_specs=(hbm,) * 6,
        scratch_shapes=[pltpu.VMEM((4, 8, LANES), f32), dma((6,))],
        compiler_params=pltpu.CompilerParams(vmem_limit_bytes=8 * 2**20),
        cost_estimate=pl.CostEstimate(flops=0, bytes_accessed=8 * rows * LANES, transcendentals=0),
        name="finish",
    )(total, master, moment, second, ff, weights)
    return (ff.reshape(grads.shape), mean, new_master, new_moment, new_second, weights.reshape(rows, LANES))


def solution(mesh):
    each, shard = P("node", "rep", None, None), P(("node", "rep"), None)
    return jax.shard_map(
        local,
        mesh=mesh,
        in_specs=(each, each, shard, shard, shard),
        out_specs=(each, shard, shard, shard, shard, P()),
        check_vma=False,
    )
```

```python
import functools

import jax
import jax.numpy as jnp
from jax import lax
from jax.experimental import pallas as pl
from jax.experimental.pallas import tpu as pltpu
from jax.sharding import PartitionSpec as P

LANES = 128
MESH = pl.DeviceIdType.MESH
ONE_BIT = 1.5 * (1.0 - 2.0**-21)


def power_of(values):
    largest = jnp.max(jnp.abs(values), axis=-1, keepdims=True)
    raised = largest * ONE_BIT
    big = raised * float(2**23)
    return (raised + big) - big


def decoded_of(values, nudge):
    scale = power_of(values)
    magic = scale * float(1.5 * 2**20)
    bound = scale * 0.875
    rounded = ((values + nudge) + magic) - magic
    return jnp.minimum(jnp.maximum(rounded, -bound), bound)


def farthest_first(size):
    return sorted(range(1, size), key=lambda off: -min(off, size - off))


def encode_master(values):
    largest = jnp.max(jnp.abs(values), axis=-1, keepdims=True)
    scale = jnp.full_like(largest, 2.0**24)
    inverse = jnp.full_like(largest, 2.0**-24)
    for k in range(23, -25, -1):
        fits = largest <= 2.0**k
        scale = jnp.where(fits, 2.0**k, scale)
        inverse = jnp.where(fits, 2.0**-k, inverse)
    code = jnp.floor(values * inverse * 128.0 + 0.5)
    code = jnp.minimum(jnp.maximum(code, -127.0), 127.0)
    return scale * code * (1.0 / 128.0)


def exchange(dims, g_hbm, f_hbm, master_ref, ff_ref, w_ref, total_ref,
             gbuf, fbuf, dbuf, sbuf, leaf, pay, out, ebuf, abuf,
             load_sem, sib_s, sib_r, leaf_s, leaf_r, pay_s, pay_r,
             az_s, az_r, ay_s, ay_r, ax_s, ax_r, ac_s, ac_r, two_s, two_r):
    Z, NX, NY, H = dims
    K = Z // 2
    R = NX * NY
    n = lax.axis_index("node")
    r = lax.axis_index("rep")
    z, c = n // 2, n % 2
    x, y = r // NY, r % NY
    oc = 1 - c

    def zoff(off):
        return lax.rem(z + off + Z, Z)

    def dev(off, core):
        return (zoff(off) * 2 + core, r)

    order = [K]
    for k in range(K - 1, 0, -1):
        order += [-k, k]
    order += [0]
    loads = {}

    def load(offs):
        for off in offs:
            d, i = zoff(off), off + K
            loads[off] = [
                pltpu.make_async_copy(g_hbm.at[d], gbuf.at[d], load_sem.at[0, i]),
                pltpu.make_async_copy(f_hbm.at[d], fbuf.at[d], load_sem.at[1, i]),
            ]
            for cp in loads[off]:
                cp.start()

    barrier = pltpu.get_barrier_semaphore()
    load(order[:1])
    for off in range(1, Z):
        pl.semaphore_signal(barrier, inc=1, device_id=dev(off, c), device_id_type=MESH)
    for off in (-1, 0, 1):
        pl.semaphore_signal(barrier, inc=1, device_id=dev(off, oc), device_id_type=MESH)
    for dx in range(NX):
        for dy in range(NY):
            if dx or dy:
                pl.semaphore_signal(barrier, inc=1, device_id_type=MESH,
                                    device_id=(n, lax.rem(x + dx, NX) * NY + lax.rem(y + dy, NY)))
    load(order[1:])

    def encode(off):
        d = zoff(off)
        for cp in loads[off]:
            cp.wait()

        xv = gbuf[d].astype(jnp.float32) + fbuf[d].astype(jnp.float32)
        dec = decoded_of(xv, 2.0**-12)
        dbuf[d] = dec.astype(jnp.bfloat16)
        ff_ref[d] = (xv - dec).astype(jnp.bfloat16)

    waits = []

    def remote(src, dst, ssem, rsem, to):
        cp = pltpu.make_async_remote_copy(
            src_ref=src, dst_ref=dst, send_sem=ssem, recv_sem=rsem, device_id=to, device_id_type=MESH
        )
        cp.start()
        waits.append(cp)
        return cp

    def level(dr, h):
        return K if dr == h else K - 1

    def sgn(dr):
        return -1 if dr == 0 else 1

    def send_leaf(dr, h):
        d = zoff(sgn(dr) * level(dr, h))
        for cc in range(2):
            remote(dbuf.at[d, cc, h], leaf.at[dr, h, c], leaf_s.at[dr, h, cc], leaf_r.at[dr, h, c],
                   dev(sgn(dr), cc))

    sib = {}

    def send_sib(off, h=None):
        d = zoff(off)
        if h is None:
            src, dst = dbuf.at[d, oc], sbuf.at[d]
        else:
            src, dst = dbuf.at[d, oc, h], sbuf.at[d, h]
        sib[off] = remote(src, dst, sib_s.at[off + K], sib_r.at[off + K], dev(0, oc))

    sib_seen = set()

    def wait_sib(off):
        if off not in sib_seen:
            sib_seen.add(off)
            sib[off].wait_recv()

    def received(dr, h, k):
        if k + 1 == level(dr, h):
            for src in range(2):
                pltpu.make_async_copy(leaf.at[dr, h, src], leaf.at[dr, h, src], leaf_r.at[dr, h, src]).wait()
            return leaf[dr, h, 0].astype(jnp.float32) + leaf[dr, h, 1].astype(jnp.float32)
        pltpu.make_async_copy(pay.at[dr, h, k], pay.at[dr, h, k], pay_r.at[dr, h, k]).wait()
        return pay[dr, h, k]

    def send_pay(dr, h, k):
        off = sgn(dr) * k
        d = zoff(off)
        wait_sib(off)
        acc = dbuf[d, c, h].astype(jnp.float32) + sbuf[d, h].astype(jnp.float32)
        out[dr, h, k] = acc + received(dr, h, k)
        remote(out.at[dr, h, k], pay.at[dr, h, k - 1], pay_s.at[dr, h, k], pay_r.at[dr, h, k - 1],
               dev(sgn(dr), c))

    w_ref[z, c, x, y] = encode_master(master_ref[...]).astype(jnp.bfloat16)
    for off in order:
        encode(off)
    pl.semaphore_wait(barrier, (Z - 1) + 3 + (R - 1))
    gz = [remote(w_ref.at[z, c, x, y], w_ref.at[z, c, x, y], az_s.at[off], az_r.at[off], dev(off, c))
          for off in farthest_first(Z)]
    send_leaf(0, 0)
    send_leaf(1, 1)
    send_sib(-(K - 1), 0)
    send_sib(K - 1, 1)
    send_leaf(0, 1)
    send_leaf(1, 0)
    for k in range(K - 2, 0, -1):
        send_sib(-k)
        send_sib(k)
    send_sib(0)
    for cp in gz:
        cp.wait_recv()
    gy = [remote(w_ref.at[:, c, x, y], w_ref.at[:, c, x, y], ay_s.at[off], ay_r.at[off],
                 (n, x * NY + lax.rem(y + off, NY))) for off in farthest_first(NY)]

    def weights_x(stage):
        def to(off):
            return (n, lax.rem(x + off + NX, NX) * NY + y)

        def piece(off, part):
            return w_ref.at[part, c, lax.rem(x + off + NX, NX)]

        full = pl.ds(0, Z)
        if stage == 0:
            for cp in gy:
                cp.wait_recv()
            for i, off in enumerate((1, -1) if NX > 2 else (1,) if NX > 1 else ()):
                gx.append(remote(piece(0, full), piece(0, full), ax_s.at[i], ax_r.at[i], to(off)))
            to_sibling(piece(0, full), 0)
        if stage == 1:
            for i, off in enumerate((1, -1) if NX > 2 else (1,) if NX > 1 else ()):
                gx[i].wait_recv()
                if NX > 2:
                    half = piece(-off, pl.ds(i * Z // 2, Z // 2))
                    gx.append(remote(half, half, ax_s.at[2 + i], ax_r.at[2 + i], to(off)))
                to_sibling(piece(-off, full), 1 + i)
        if stage == 2 and NX > 2:
            for cp in gx[2:]:
                cp.wait_recv()
            to_sibling(piece(2, full), 3)

    def to_sibling(ref, i):
        gc.append(remote(ref, ref, ac_s.at[i], ac_r.at[i], dev(0, oc)))

    gx, gc = [], []
    for k in range(K - 1, 0, -1):
        for second in (True, False):
            for dr in range(2):
                h = dr if not second else 1 - dr
                if k < level(dr, h):
                    send_pay(dr, h, k)
            if k == 1 and second:
                weights_x(0)

    G = R // 2
    wait_sib(0)
    for h in (1, 0):
        part = dbuf[z, c, h].astype(jnp.float32) + sbuf[z, h].astype(jnp.float32)
        part = part + received(0, h, 0) + received(1, h, 0)
        two = decoded_of(part, 2.0**-15)
        ebuf[h * G:(h + 1) * G] = two.reshape(G, 8, LANES).astype(jnp.bfloat16)

        for j in range(NY):
            dy = NY // 2 + (1 - 2 * (j % 2)) * ((j + 1) // 2)
            for i in range(NX // 2):
                to = (h * NX // 2 + i) * NY + lax.rem(y + dy, NY)

                def send():
                    pltpu.make_async_remote_copy(
                        src_ref=ebuf.at[to], dst_ref=abuf.at[r], send_sem=two_s, recv_sem=two_r,
                        device_id=(n, to), device_id_type=MESH).start()

                if dy == 0:
                    pl.when(to != r)(send)
                else:
                    send()

    weights_x(1)
    abuf[r] = ebuf[r]
    rest = abuf.at[pl.ds(0, R - 1)]
    pltpu.make_async_copy(rest, rest, two_r).wait()
    total_ref[...] = jnp.sum(abuf[...].astype(jnp.float32), axis=0)
    weights_x(2)
    for cp in gc:
        cp.wait_recv()
    for cp in waits:
        cp.wait_send()
    pltpu.make_async_copy(rest, rest, two_s).wait()


def finish(devices, total_ref, master_ref, moment_ref, second_ref, ff_in, w_in,
           ff_out, mean_out, master_out, moment_out, second_out, w_out, small, sem):
    copies = [pltpu.make_async_copy(ff_in, ff_out, sem.at[4]), pltpu.make_async_copy(w_in, w_out, sem.at[5])]
    for cp in copies:
        cp.start()
    mean = total_ref[...] * (1.0 / devices)
    master = master_ref[...]
    moment = 0.9 * moment_ref[...] + 0.1 * mean
    second = 0.95 * second_ref[...] + 0.05 * mean * mean
    update = moment / 0.6513216 / (jnp.sqrt(second / 0.4012631) + 1e-08)
    small[0] = mean
    small[1] = master - 0.01 * (update + 0.1 * master)
    small[2] = moment
    small[3] = second
    for i, out in enumerate((mean_out, master_out, moment_out, second_out)):
        copies.append(pltpu.make_async_copy(small.at[i], out, sem.at[i]))
        copies[-1].start()
    for cp in copies:
        cp.wait()


def local(grads, feedback, master, moment, second):
    nodes, R = lax.axis_size("node"), lax.axis_size("rep")
    rows = grads.shape[2]
    Z = nodes // 2
    K = Z // 2
    NX = {32: 4, 4: 2}.get(R, 1)
    NY = R // NX
    H = rows // nodes // 2
    bf, f32 = jnp.bfloat16, jnp.float32
    blocks = (Z, 2, 2, H, LANES)
    wshape = (Z, 2, NX, NY, 8, LANES)
    hbm, vmem = pl.BlockSpec(memory_space=pltpu.HBM), pl.BlockSpec(memory_space=pltpu.VMEM)
    dma = pltpu.SemaphoreType.DMA
    ff, weights, total = pl.pallas_call(
        functools.partial(exchange, (Z, NX, NY, H)),
        out_shape=(
            jax.ShapeDtypeStruct(blocks, bf),
            jax.ShapeDtypeStruct(wshape, bf),
            jax.ShapeDtypeStruct((8, LANES), f32),
        ),
        in_specs=[hbm, hbm, vmem],
        out_specs=(vmem, vmem, vmem),
        scratch_shapes=[
            pltpu.VMEM(blocks, bf),
            pltpu.VMEM(blocks, bf),
            pltpu.VMEM(blocks, bf),
            pltpu.VMEM((Z, 2, H, LANES), bf),
            pltpu.VMEM((2, 2, 2, H, LANES), bf),
            pltpu.VMEM((2, 2, K, H, LANES), f32),
            pltpu.VMEM((2, 2, K, H, LANES), f32),
            pltpu.VMEM((R, 8, LANES), bf),
            pltpu.VMEM((R, 8, LANES), bf),
            dma((2, Z + 1)),
            dma((Z + 1,)), dma((Z + 1,)),
            dma((2, 2, 2)), dma((2, 2, 2)),
            dma((2, 2, K)), dma((2, 2, K)),
            dma((Z,)), dma((Z,)),
            dma((NY,)), dma((NY,)),
            dma((4,)), dma((4,)),
            dma((4,)), dma((4,)),
            dma, dma,
        ],
        compiler_params=pltpu.CompilerParams(
            collective_id=0, has_side_effects=True, vmem_limit_bytes=51 * 2**20 + 2**19
        ),
        cost_estimate=pl.CostEstimate(flops=20 * rows * LANES, bytes_accessed=10 * rows * LANES, transcendentals=0),
        name="exchange",
    )(grads.reshape(blocks), feedback.reshape(blocks), master)
    shard = jax.ShapeDtypeStruct((8, LANES), f32)
    ff, mean, new_master, new_moment, new_second, weights = pl.pallas_call(
        functools.partial(finish, nodes * R),
        out_shape=(jax.ShapeDtypeStruct(blocks, bf), shard, shard, shard, shard, jax.ShapeDtypeStruct(wshape, bf)),
        in_specs=[vmem] * 6,
        out_specs=(hbm,) * 6,
        scratch_shapes=[pltpu.VMEM((4, 8, LANES), f32), dma((6,))],
        compiler_params=pltpu.CompilerParams(vmem_limit_bytes=8 * 2**20),
        cost_estimate=pl.CostEstimate(flops=0, bytes_accessed=8 * rows * LANES, transcendentals=0),
        name="finish",
    )(total, master, moment, second, ff, weights)
    return (ff.reshape(grads.shape), mean, new_master, new_moment, new_second, weights.reshape(rows, LANES))


def solution(mesh):
    each, shard = P("node", "rep", None, None), P(("node", "rep"), None)
    return jax.shard_map(
        local,
        mesh=mesh,
        in_specs=(each, each, shard, shard, shard),
        out_specs=(each, shard, shard, shard, shard, P()),
        check_vma=False,
    )
```

```python
import functools

import jax
import jax.numpy as jnp
from jax import lax
from jax.experimental import pallas as pl
from jax.experimental.pallas import tpu as pltpu
from jax.sharding import PartitionSpec as P

LANES = 128
MESH = pl.DeviceIdType.MESH
ONE_BIT = 1.5 * (1.0 - 2.0**-21)


def power_of(values):
    largest = jnp.max(jnp.abs(values), axis=-1, keepdims=True)
    raised = largest * ONE_BIT
    big = raised * float(2**23)
    return (raised + big) - big


def decoded_of(values, nudge):
    scale = power_of(values)
    magic = scale * float(1.5 * 2**20)
    bound = scale * 0.875
    rounded = ((values + nudge) + magic) - magic
    return jnp.minimum(jnp.maximum(rounded, -bound), bound)


def farthest_first(size):
    return sorted(range(1, size), key=lambda off: -min(off, size - off))


def encode_master(values):
    largest = jnp.max(jnp.abs(values), axis=-1, keepdims=True)
    scale = jnp.full_like(largest, 2.0**24)
    inverse = jnp.full_like(largest, 2.0**-24)
    for k in range(23, -25, -1):
        fits = largest <= 2.0**k
        scale = jnp.where(fits, 2.0**k, scale)
        inverse = jnp.where(fits, 2.0**-k, inverse)
    code = jnp.floor(values * inverse * 128.0 + 0.5)
    code = jnp.minimum(jnp.maximum(code, -127.0), 127.0)
    return scale * code * (1.0 / 128.0)


def exchange(dims, g_hbm, f_hbm, master_ref, ff_ref, w_ref, total_ref,
             gbuf, fbuf, dbuf, sbuf, leaf, pay, out, ebuf, abuf,
             load_sem, sib_s, sib_r, leaf_s, leaf_r, pay_s, pay_r,
             az_s, az_r, ay_s, ay_r, ax_s, ax_r, ac_s, ac_r, two_s, two_r):
    Z, NX, NY, H = dims
    K = Z // 2
    R = NX * NY
    n = lax.axis_index("node")
    r = lax.axis_index("rep")
    z, c = n // 2, n % 2
    x, y = r // NY, r % NY
    oc = 1 - c

    def zoff(off):
        return lax.rem(z + off + Z, Z)

    def dev(off, core):
        return (zoff(off) * 2 + core, r)

    order = [K]
    for k in range(K - 1, 0, -1):
        order += [-k, k]
    order += [0]
    loads = {}

    def load(offs):
        for off in offs:
            d, i = zoff(off), off + K
            loads[off] = [
                pltpu.make_async_copy(g_hbm.at[d], gbuf.at[d], load_sem.at[0, i]),
                pltpu.make_async_copy(f_hbm.at[d], fbuf.at[d], load_sem.at[1, i]),
            ]
            for cp in loads[off]:
                cp.start()

    barrier = pltpu.get_barrier_semaphore()
    load(order[:1])
    for off in range(1, Z):
        pl.semaphore_signal(barrier, inc=1, device_id=dev(off, c), device_id_type=MESH)
    for off in (-1, 0, 1):
        pl.semaphore_signal(barrier, inc=1, device_id=dev(off, oc), device_id_type=MESH)
    for dx in range(NX):
        for dy in range(NY):
            if dx or dy:
                pl.semaphore_signal(barrier, inc=1, device_id_type=MESH,
                                    device_id=(n, lax.rem(x + dx, NX) * NY + lax.rem(y + dy, NY)))
    load(order[1:])

    def encode(off):
        d = zoff(off)
        for cp in loads[off]:
            cp.wait()

        xv = gbuf[d].astype(jnp.float32) + fbuf[d].astype(jnp.float32)
        dec = decoded_of(xv, 2.0**-12)
        dbuf[d] = dec.astype(jnp.bfloat16)
        ff_ref[d] = (xv - dec).astype(jnp.bfloat16)

    waits = []

    def remote(src, dst, ssem, rsem, to):
        cp = pltpu.make_async_remote_copy(
            src_ref=src, dst_ref=dst, send_sem=ssem, recv_sem=rsem, device_id=to, device_id_type=MESH
        )
        cp.start()
        waits.append(cp)
        return cp

    def level(dr, h):
        return K if dr == h else K - 1

    def sgn(dr):
        return -1 if dr == 0 else 1

    def send_leaf(dr, h):
        d = zoff(sgn(dr) * level(dr, h))
        for cc in range(2):
            remote(dbuf.at[d, cc, h], leaf.at[dr, h, c], leaf_s.at[dr, h, cc], leaf_r.at[dr, h, c],
                   dev(sgn(dr), cc))

    sib = {}

    def send_sib(off, h=None):
        d = zoff(off)
        if h is None:
            src, dst = dbuf.at[d, oc], sbuf.at[d]
        else:
            src, dst = dbuf.at[d, oc, h], sbuf.at[d, h]
        sib[off] = remote(src, dst, sib_s.at[off + K], sib_r.at[off + K], dev(0, oc))

    sib_seen = set()

    def wait_sib(off):
        if off not in sib_seen:
            sib_seen.add(off)
            sib[off].wait_recv()

    def received(dr, h, k):
        if k + 1 == level(dr, h):
            for src in range(2):
                pltpu.make_async_copy(leaf.at[dr, h, src], leaf.at[dr, h, src], leaf_r.at[dr, h, src]).wait()
            return leaf[dr, h, 0].astype(jnp.float32) + leaf[dr, h, 1].astype(jnp.float32)
        pltpu.make_async_copy(pay.at[dr, h, k], pay.at[dr, h, k], pay_r.at[dr, h, k]).wait()
        return pay[dr, h, k]

    def send_pay(dr, h, k):
        off = sgn(dr) * k
        d = zoff(off)
        wait_sib(off)
        acc = dbuf[d, c, h].astype(jnp.float32) + sbuf[d, h].astype(jnp.float32)
        out[dr, h, k] = acc + received(dr, h, k)
        remote(out.at[dr, h, k], pay.at[dr, h, k - 1], pay_s.at[dr, h, k], pay_r.at[dr, h, k - 1],
               dev(sgn(dr), c))

    w_ref[z, c, x, y] = encode_master(master_ref[...]).astype(jnp.bfloat16)
    for off in order:
        encode(off)
    pl.semaphore_wait(barrier, (Z - 1) + 3 + (R - 1))
    gz = [remote(w_ref.at[z, c, x, y], w_ref.at[z, c, x, y], az_s.at[off], az_r.at[off], dev(off, c))
          for off in farthest_first(Z)]
    send_leaf(0, 0)
    send_leaf(1, 1)
    send_sib(-(K - 1), 0)
    send_sib(K - 1, 1)
    send_leaf(0, 1)
    send_leaf(1, 0)
    for k in range(K - 2, 0, -1):
        send_sib(-k)
        send_sib(k)
    send_sib(0)
    for cp in gz:
        cp.wait_recv()
    gy = [remote(w_ref.at[:, c, x, y], w_ref.at[:, c, x, y], ay_s.at[off], ay_r.at[off],
                 (n, x * NY + lax.rem(y + off, NY))) for off in farthest_first(NY)]

    def weights_x(stage):
        def to(off):
            return (n, lax.rem(x + off + NX, NX) * NY + y)

        def piece(off, part):
            return w_ref.at[part, c, lax.rem(x + off + NX, NX)]

        full = pl.ds(0, Z)
        if stage == 0:
            for cp in gy:
                cp.wait_recv()
            for i, off in enumerate((1, -1) if NX > 2 else (1,) if NX > 1 else ()):
                gx.append(remote(piece(0, full), piece(0, full), ax_s.at[i], ax_r.at[i], to(off)))
            to_sibling(piece(0, full), 0)
        if stage == 1:
            for i, off in enumerate((1, -1) if NX > 2 else (1,) if NX > 1 else ()):
                gx[i].wait_recv()
                if NX > 2:
                    half = piece(-off, pl.ds(i * Z // 2, Z // 2))
                    gx.append(remote(half, half, ax_s.at[2 + i], ax_r.at[2 + i], to(off)))
                to_sibling(piece(-off, full), 1 + i)
        if stage == 2 and NX > 2:
            for cp in gx[2:]:
                cp.wait_recv()
            to_sibling(piece(2, full), 3)

    def to_sibling(ref, i):
        gc.append(remote(ref, ref, ac_s.at[i], ac_r.at[i], dev(0, oc)))

    gx, gc = [], []
    for k in range(K - 1, 0, -1):
        for second in (True, False):
            for dr in range(2):
                h = dr if not second else 1 - dr
                if k < level(dr, h):
                    send_pay(dr, h, k)
            if k == 1 and second:
                weights_x(0)

    wait_sib(0)
    parts = []
    for h in range(2):
        part = dbuf[z, c, h].astype(jnp.float32) + sbuf[z, h].astype(jnp.float32)
        part = part + received(0, h, 0) + received(1, h, 0)
        parts.append(part)
    two = decoded_of(jnp.concatenate(parts, axis=0), 2.0**-15)
    ebuf[...] = two.reshape(R, 8, LANES).astype(jnp.bfloat16)
    for j in range(NY):
        dy = NY // 2 + (1 - 2 * (j % 2)) * ((j + 1) // 2)
        for i in range(NX):
            to = i * NY + lax.rem(y + dy, NY)

            def send():
                pltpu.make_async_remote_copy(
                    src_ref=ebuf.at[to], dst_ref=abuf.at[r], send_sem=two_s, recv_sem=two_r,
                    device_id=(n, to), device_id_type=MESH).start()

            if dy == 0:
                pl.when(to != r)(send)
            else:
                send()

    weights_x(1)
    abuf[r] = ebuf[r]
    rest = abuf.at[pl.ds(0, R - 1)]
    pltpu.make_async_copy(rest, rest, two_r).wait()
    total_ref[...] = jnp.sum(abuf[...].astype(jnp.float32), axis=0)
    weights_x(2)
    for cp in gc:
        cp.wait_recv()
    for cp in waits:
        cp.wait_send()
    pltpu.make_async_copy(rest, rest, two_s).wait()


def finish(devices, total_ref, master_ref, moment_ref, second_ref, ff_in, w_in,
           ff_out, mean_out, master_out, moment_out, second_out, w_out, small, sem):
    copies = [pltpu.make_async_copy(ff_in, ff_out, sem.at[4]), pltpu.make_async_copy(w_in, w_out, sem.at[5])]
    for cp in copies:
        cp.start()
    mean = total_ref[...] * (1.0 / devices)
    master = master_ref[...]
    moment = 0.9 * moment_ref[...] + 0.1 * mean
    second = 0.95 * second_ref[...] + 0.05 * mean * mean
    update = moment / 0.6513216 / (jnp.sqrt(second / 0.4012631) + 1e-08)
    small[0] = mean
    small[1] = master - 0.01 * (update + 0.1 * master)
    small[2] = moment
    small[3] = second
    for i, out in enumerate((mean_out, master_out, moment_out, second_out)):
        copies.append(pltpu.make_async_copy(small.at[i], out, sem.at[i]))
        copies[-1].start()
    for cp in copies:
        cp.wait()


def local(grads, feedback, master, moment, second):
    nodes, R = lax.axis_size("node"), lax.axis_size("rep")
    rows = grads.shape[2]
    Z = nodes // 2
    K = Z // 2
    NX = {32: 4, 4: 2}.get(R, 1)
    NY = R // NX
    H = rows // nodes // 2
    bf, f32 = jnp.bfloat16, jnp.float32
    blocks = (Z, 2, 2, H, LANES)
    wshape = (Z, 2, NX, NY, 8, LANES)
    hbm, vmem = pl.BlockSpec(memory_space=pltpu.HBM), pl.BlockSpec(memory_space=pltpu.VMEM)
    dma = pltpu.SemaphoreType.DMA
    ff, weights, total = pl.pallas_call(
        functools.partial(exchange, (Z, NX, NY, H)),
        out_shape=(
            jax.ShapeDtypeStruct(blocks, bf),
            jax.ShapeDtypeStruct(wshape, bf),
            jax.ShapeDtypeStruct((8, LANES), f32),
        ),
        in_specs=[hbm, hbm, vmem],
        out_specs=(vmem, vmem, vmem),
        scratch_shapes=[
            pltpu.VMEM(blocks, bf),
            pltpu.VMEM(blocks, bf),
            pltpu.VMEM(blocks, bf),
            pltpu.VMEM((Z, 2, H, LANES), bf),
            pltpu.VMEM((2, 2, 2, H, LANES), bf),
            pltpu.VMEM((2, 2, K, H, LANES), f32),
            pltpu.VMEM((2, 2, K, H, LANES), f32),
            pltpu.VMEM((R, 8, LANES), bf),
            pltpu.VMEM((R, 8, LANES), bf),
            dma((2, Z + 1)),
            dma((Z + 1,)), dma((Z + 1,)),
            dma((2, 2, 2)), dma((2, 2, 2)),
            dma((2, 2, K)), dma((2, 2, K)),
            dma((Z,)), dma((Z,)),
            dma((NY,)), dma((NY,)),
            dma((4,)), dma((4,)),
            dma((4,)), dma((4,)),
            dma, dma,
        ],
        compiler_params=pltpu.CompilerParams(
            collective_id=0, has_side_effects=True, vmem_limit_bytes=51 * 2**20 + 2**19
        ),
        cost_estimate=pl.CostEstimate(flops=20 * rows * LANES, bytes_accessed=10 * rows * LANES, transcendentals=0),
        name="exchange",
    )(grads.reshape(blocks), feedback.reshape(blocks), master)
    shard = jax.ShapeDtypeStruct((8, LANES), f32)
    ff, mean, new_master, new_moment, new_second, weights = pl.pallas_call(
        functools.partial(finish, nodes * R),
        out_shape=(jax.ShapeDtypeStruct(blocks, bf), shard, shard, shard, shard, jax.ShapeDtypeStruct(wshape, bf)),
        in_specs=[vmem] * 6,
        out_specs=(hbm,) * 6,
        scratch_shapes=[pltpu.VMEM((4, 8, LANES), f32), dma((6,))],
        compiler_params=pltpu.CompilerParams(vmem_limit_bytes=8 * 2**20),
        cost_estimate=pl.CostEstimate(flops=0, bytes_accessed=8 * rows * LANES, transcendentals=0),
        name="finish",
    )(total, master, moment, second, ff, weights)
    return (ff.reshape(grads.shape), mean, new_master, new_moment, new_second, weights.reshape(rows, LANES))


def solution(mesh):
    each, shard = P("node", "rep", None, None), P(("node", "rep"), None)
    return jax.shard_map(
        local,
        mesh=mesh,
        in_specs=(each, each, shard, shard, shard),
        out_specs=(each, shard, shard, shard, shard, P()),
        check_vma=False,
    )
```
